512 devices in a mesh: gx: 16 (over y_lo, x), gy: 32 (over y_hi, z, core).
Axes of the slice: x: 4, y: 8 (y_hi: 2, y_lo: 4; y = y_hi * 4 + y_lo), z: 8, core: 2. Of those that a mesh axis runs over, the one named last changes fastest.
Arguments:
- grid_field: float32 [128, 1024, 512], P('gy', 'gx'), may hold values from -6 to 6
- operator_blocks: float32 [16, 512, 4, 2, 1024], P('gx', 'gy'), may hold values from -0.75 to 0.75
- op_columns: int32 [16, 512, 4, 2], P('gx', 'gy'), may hold values from 0 to 3, as said below
- diag_inverse: float32 [16, 512, 2, 4, 1024], P('gx', 'gy'), may hold values from -3 to 3
- off_blocks: float32 [16, 512, 2, 3, 1024], P('gx', 'gy'), may hold values from -0.5 to 0.5
Outputs:
- advanced_field: float32 [128, 1024, 512], P('gy', 'gx')
The draws below stay inside these ranges and needn't reach their ends.
Inputs may be any that keep to these rules, and one draw needn't show every extreme that they name: `op_columns`: for every group and block row, slot 0 names the block row itself and slot 1 another block row within two of it.
All inputs are finite; a program needn't handle non-finite values.
Results may differ from the reference program's by a relative error of at most 0.0001.
Values sent between devices are 32-bit elements; how exact they have to be, the bound alone decides.
No kernel may reach another device: no remote copies, remote signals or barrier semaphores. Data moves between devices by JAX's collectives and lax.ppermute only.
A program may use at most 64 MiB of HBM per device.

```python
import math
import jax
import jax.numpy as jnp
from jax import lax

NX = 512
NY = 1024
NZ = 128
CHEBYSHEV_ROWS = 32
KXG = 16
STORED_BLOCKS = 2
KX = 256
VERTICAL_BLOCKS = 4
X_MODE_GROUPS = 16
Y_MODE_GROUPS = 512


def draw_op_columns(key, part):
    key = jax.random.fold_in(key, 11)
    steps_drawn = jax.random.randint(key, (X_MODE_GROUPS, Y_MODE_GROUPS, VERTICAL_BLOCKS), 0, 4)
    offsets = jnp.where(steps_drawn < 2, steps_drawn - 2, steps_drawn - 1).astype(jnp.int32)
    diagonal_rows = jnp.broadcast_to(jnp.arange(VERTICAL_BLOCKS, dtype=jnp.int32), (X_MODE_GROUPS, Y_MODE_GROUPS, VERTICAL_BLOCKS))
    other_rows = diagonal_rows + offsets
    outside = jnp.logical_or(other_rows < 0, other_rows >= VERTICAL_BLOCKS)
    other_rows = jnp.where(outside, diagonal_rows - offsets, other_rows)
    return jnp.stack([diagonal_rows, other_rows], axis=-1).astype(jnp.int32)


def draw_diag_inverse(key, part):
    key = jax.random.fold_in(key, 23)
    shape_full = (X_MODE_GROUPS, Y_MODE_GROUPS, 2, VERTICAL_BLOCKS, CHEBYSHEV_ROWS, CHEBYSHEV_ROWS)
    noise = jnp.clip(jax.random.normal(key, shape_full, jnp.float32), -4.0, 4.0)
    identity = jnp.eye(CHEBYSHEV_ROWS, dtype=jnp.float32)
    blocks_all = identity + noise * (0.5 / math.sqrt(CHEBYSHEV_ROWS))
    return blocks_all.reshape(X_MODE_GROUPS, Y_MODE_GROUPS, 2, VERTICAL_BLOCKS, CHEBYSHEV_ROWS * CHEBYSHEV_ROWS)


def levels(rng, shape, cuts, smallest, top_value):
    def one(axis_at, parts):
        heights = jax.random.uniform(jax.random.fold_in(jax.random.fold_in(rng, 6), axis_at), (parts,), jnp.float32, smallest / len(cuts), top_value / len(cuts))
        return jnp.repeat(jnp.exp(heights), shape[axis_at] // parts).reshape((-1,) + (1,) * (len(shape) - axis_at - 1))

    loudness = one(*cuts[0])
    for cut in cuts[1:]:
        loudness = loudness * one(*cut)
    return loudness


def gaussian(stream_key, shape, scale, limit, cuts=(), kind=jnp.bfloat16):
    array = jax.random.normal(stream_key, shape, jnp.float32) * scale
    if len(cuts) > 0:
        array = levels(stream_key, shape, cuts, -0.22, 0.18) * array
    return jnp.clip(array, min=-limit, max=limit).astype(kind)


def setup_inputs(seed: int = 0) -> dict:
    key_of = jax.random.split(jax.random.key(seed), 6)
    return {
        "grid_field": gaussian(key_of[0], (NZ, NY, NX), 1.0, 6.0, ((0, 32), (1, 16)), jnp.float32),
        "operator_blocks": gaussian(key_of[1], (X_MODE_GROUPS, Y_MODE_GROUPS, VERTICAL_BLOCKS, STORED_BLOCKS, CHEBYSHEV_ROWS * CHEBYSHEV_ROWS), (2 * CHEBYSHEV_ROWS) ** -0.5, 0.75, ((0, 16), (1, 32)), jnp.float32),
        "op_columns": draw_op_columns(jax.random.fold_in(key_of[5], 71), 0),
        "diag_inverse": draw_diag_inverse(jax.random.fold_in(key_of[5], 71), 0),
        "off_blocks": gaussian(key_of[4], (X_MODE_GROUPS, Y_MODE_GROUPS, 2, VERTICAL_BLOCKS - 1, CHEBYSHEV_ROWS * CHEBYSHEV_ROWS), (4 * CHEBYSHEV_ROWS) ** -0.5, 0.5, ((0, 16), (1, 32)), jnp.float32),
    }


precise_mode = lax.Precision.HIGHEST

def solve_group(pieces):
    columns, weight_values, picks, inverses, coupling = pieces
    chosen = jnp.einsum('yisj,jbym->isbym', picks, columns, precision=precise_mode)
    applied = jnp.einsum('yisab,isbym->iaym', weight_values, chosen, precision=precise_mode)

    def apply_block(matrix, target):
        return jnp.einsum('yab,bym->aym', matrix, target, precision=precise_mode)
    running = apply_block(inverses[:, 0, 0], applied[0])
    forward_part = [running]
    for block_row in range(1, VERTICAL_BLOCKS):
        running = apply_block(inverses[:, 0, block_row], applied[block_row] - apply_block(coupling[:, 0, block_row - 1], running))
        forward_part.append(running)
    backward_part = [forward_part[0]] * VERTICAL_BLOCKS
    running = apply_block(inverses[:, 1, VERTICAL_BLOCKS - 1], forward_part[VERTICAL_BLOCKS - 1])
    backward_part[VERTICAL_BLOCKS - 1] = running
    for block_row in range(VERTICAL_BLOCKS - 2, -1, -1):
        running = apply_block(inverses[:, 1, block_row], forward_part[block_row] - apply_block(coupling[:, 1, block_row], running))
        backward_part[block_row] = running
    return jnp.stack(backward_part, axis=0)

def reference(grid_field, operator_blocks, op_columns, diag_inverse, off_blocks):
    spectral_x = jnp.fft.rfft(grid_field, axis=2)[:, :, :KX] / math.sqrt(NX)
    spectral = jnp.fft.fft(spectral_x, axis=1) / math.sqrt(NY)
    stacked = jnp.stack([jnp.real(spectral), jnp.imag(spectral)], axis=-1).astype(jnp.float32)
    grouped = stacked.reshape(VERTICAL_BLOCKS, CHEBYSHEV_ROWS, Y_MODE_GROUPS, 2, X_MODE_GROUPS, KXG, 2).transpose(4, 0, 1, 2, 3, 5, 6)
    grouped = grouped.reshape(X_MODE_GROUPS, VERTICAL_BLOCKS, CHEBYSHEV_ROWS, Y_MODE_GROUPS, 4 * KXG)
    picks = (op_columns[..., None] == jnp.arange(VERTICAL_BLOCKS, dtype=jnp.int32)).astype(jnp.float32)
    weight_values = operator_blocks.reshape(X_MODE_GROUPS, Y_MODE_GROUPS, VERTICAL_BLOCKS, STORED_BLOCKS, CHEBYSHEV_ROWS, CHEBYSHEV_ROWS)
    inverses = diag_inverse.reshape(X_MODE_GROUPS, Y_MODE_GROUPS, 2, VERTICAL_BLOCKS, CHEBYSHEV_ROWS, CHEBYSHEV_ROWS)
    coupling = off_blocks.reshape(X_MODE_GROUPS, Y_MODE_GROUPS, 2, VERTICAL_BLOCKS - 1, CHEBYSHEV_ROWS, CHEBYSHEV_ROWS)
    solved = lax.map(solve_group, (grouped, weight_values, picks, inverses, coupling))
    ungrouped = solved.reshape(X_MODE_GROUPS, VERTICAL_BLOCKS, CHEBYSHEV_ROWS, Y_MODE_GROUPS, 2, KXG, 2).transpose(1, 2, 3, 4, 0, 5, 6)
    ungrouped = ungrouped.reshape(NZ, NY, KX, 2)
    complex_back = lax.complex(ungrouped[..., 0], ungrouped[..., 1])
    rows_back = jnp.fft.ifft(complex_back, axis=1) * math.sqrt(NY)
    padded = jnp.concatenate([rows_back, jnp.zeros((NZ, NY, 1), rows_back.dtype)], axis=2)
    advanced_field = jnp.fft.irfft(padded, n=NX, axis=2) * math.sqrt(NX)
    return advanced_field.astype(jnp.float32)
```

```python
import math

import jax
import jax.numpy as jnp
import ml_dtypes
import numpy as np
from jax import lax
from jax.experimental import pallas as pl
from jax.experimental.pallas import tpu as pltpu
from jax.sharding import PartitionSpec as P

NX = 512
NY = 1024
QUARTER = NY // 4
HALF = NX // 2
LANES = 128
SPAN = 16
BLOCK = 32
PART = SPAN // 2
VMEM_LIMIT = 24 * 1024 * 1024

f32 = jnp.float32
bf16 = jnp.bfloat16


def split_table(table):
    high = table.astype(ml_dtypes.bfloat16)
    low = (table - high.astype(np.float64)).astype(ml_dtypes.bfloat16)
    return high, low


def x_tables():
    parity = np.arange(2).reshape(2, 1, 1)
    x = np.arange(HALF).reshape(1, HALF, 1)
    k = 2 * np.arange(HALF // 2).reshape(1, 1, HALF // 2) + parity
    angle = (x * k % NX) * (2.0 * math.pi / NX)
    shape = (2, HALF, HALF // SPAN, PART)
    cosine = np.cos(angle).reshape(shape) / math.sqrt(NX)
    sine = np.sin(angle).reshape(shape) / math.sqrt(NX)
    forward = np.stack([cosine, -sine], axis=3)
    weight = np.where(k == 0, 1.0, 2.0).reshape(2, 1, HALF // SPAN, 1, PART)
    backward = (forward * weight).reshape(2, HALF, HALF).transpose(0, 2, 1)
    return split_table(forward.reshape(2, HALF, HALF)), split_table(backward)


def y_tables():
    q1 = np.arange(4).reshape(4, 1, 1)
    q2 = np.arange(QUARTER).reshape(1, QUARTER, 1)
    y2 = np.arange(QUARTER).reshape(1, 1, QUARTER)
    angle = ((q1 + 4 * q2) * y2 % NY) * (2.0 * math.pi / NY)
    cosine = np.cos(angle) / math.sqrt(NY)
    sine = np.sin(angle) / math.sqrt(NY)
    forward = np.concatenate([cosine, sine], axis=2)
    backward = np.concatenate([cosine.transpose(0, 2, 1), -sine.transpose(0, 2, 1)], axis=2)
    return split_table(forward), split_table(backward)


def split(values):
    high = values.astype(bf16)
    low = (values - high.astype(f32)).astype(bf16)
    return high, low


def mul(left, right):
    return jnp.dot(left, right, preferred_element_type=f32)


def lane_index(shape):
    return lax.broadcasted_iota(jnp.int32, shape, len(shape) - 1)


def swap_groups(parts):
    parts = list(parts)
    lane = lane_index(parts[0].shape)
    distance, reach = len(parts) // 2, LANES // 2
    while distance:
        first = (lane & reach) == 0
        for i in range(len(parts)):
            if not i & distance:
                a, b = parts[i], parts[i + distance]
                parts[i] = jnp.where(first, a, pltpu.roll(b, reach, 1))
                parts[i + distance] = jnp.where(first, pltpu.roll(a, LANES - reach, 1), b)
        distance, reach = distance // 2, reach // 2
    return parts


def turned(values):
    real = (lane_index(values.shape) & PART) == 0
    return jnp.where(real, pltpu.roll(values, LANES - PART, 1), -pltpu.roll(values, PART, 1))


def x_forward_kernel(grid_hbm, high_hbm, low_hbm, out_ref, grid_ref, high_ref, low_ref, sems):
    depth, lines, length = grid_ref.shape
    pairs = [(high_hbm, high_ref), (low_hbm, low_ref)]
    pairs += [(grid_hbm.at[z], grid_ref.at[z]) for z in range(depth)]
    copies = [
        pltpu.make_async_copy(source, target, sems.at[i])
        for i, (source, target) in enumerate(pairs)
    ]
    for copy in copies:
        copy.start()
    for copy in copies:
        copy.wait()
    near = grid_ref[:, :, :HALF].reshape(depth * lines, HALF)
    far = grid_ref[:, :, HALF:].reshape(depth * lines, HALF)
    sums = []
    for p, values in enumerate((near + far, near - far)):
        high, low = split(values)
        wide = mul(jnp.concatenate([high, low], axis=0), high_ref[p])
        sums.append(wide[: depth * lines] + (wide[depth * lines :] + mul(high, low_ref[p])))
    for a in range(HALF // LANES):
        columns = slice(a * LANES, (a + 1) * LANES)
        parts = [
            sums[p][z * lines : (z + 1) * lines, columns] for z in range(depth) for p in range(2)
        ]
        for b, part in enumerate(swap_groups(parts)):
            out_ref[8 * a + b] = part


def x_backward_kernel(in_ref, high_ref, low_ref, out_ref):
    depth, lines, length = out_ref.shape
    columns = [swap_groups([in_ref[8 * a + b] for b in range(8)]) for a in range(HALF // LANES)]
    results = []
    for p in range(2):
        rows = [
            jnp.concatenate([column[2 * z + p] for column in columns], axis=1)
            for z in range(depth)
        ]
        high, low = split(jnp.concatenate(rows, axis=0))
        wide = mul(jnp.concatenate([high, low], axis=0), high_ref[p])
        results.append(wide[: depth * lines] + (wide[depth * lines :] + mul(high, low_ref[p])))
    near, far = results
    out_ref[:, :, :HALF] = (near + far).reshape(depth, lines, HALF)
    out_ref[:, :, HALF:] = (near - far).reshape(depth, lines, HALF)


def quarter_product(values, high_table, low_table):
    both = jnp.concatenate([values, turned(values)], axis=0)
    high, low = split(both)
    wide = mul(high_table, jnp.concatenate([high, low], axis=1))
    return wide[:, :LANES] + (wide[:, LANES:] + mul(low_table, high))


def y_forward_kernel(in_ref, high_ref, low_ref, out_ref):
    a, b, c, d = [in_ref[i * QUARTER : (i + 1) * QUARTER, :] for i in range(4)]
    even_sum, even_difference = a + c, a - c
    odd_sum, odd_difference = b + d, turned(b - d)
    mixed = (
        even_sum + odd_sum,
        even_difference + odd_difference,
        even_sum - odd_sum,
        even_difference - odd_difference,
    )
    for q1 in range(4):
        result = quarter_product(mixed[q1], high_ref[q1], low_ref[q1])
        out_ref[:, 8 * q1 : 8 * q1 + 8, :] = result.reshape(QUARTER // 8, 8, LANES)


def y_backward_kernel(in_ref, high_ref, low_ref, out_ref):
    products = []
    for q1 in range(4):
        values = in_ref[:, 8 * q1 : 8 * q1 + 8, :].reshape(QUARTER, LANES)
        products.append(quarter_product(values, high_ref[q1], low_ref[q1]))
    a, b, c, d = products
    even_sum, even_difference = a + c, a - c
    odd_sum, odd_difference = b + d, turned(b - d)
    out_ref[0:QUARTER, :] = even_sum + odd_sum
    out_ref[QUARTER : 2 * QUARTER, :] = even_difference - odd_difference
    out_ref[2 * QUARTER : 3 * QUARTER, :] = even_sum - odd_sum
    out_ref[3 * QUARTER :, :] = even_difference + odd_difference


def spread_left(matrix):
    rest = matrix - matrix.astype(bf16).astype(f32)
    return jnp.concatenate([matrix, rest, matrix], axis=1).astype(bf16)


def three(matrix, right):
    high, low = split(right)
    return mul(spread_left(matrix), jnp.concatenate([high, high, low], axis=0))


def operator_kernel(columns_ref, blocks_ref, diag_ref, off_ref, out_ref, hold_ref):
    groups = blocks_ref.shape[0]
    lane = lane_index((BLOCK, LANES))
    row = lax.broadcasted_iota(jnp.int32, (BLOCK, LANES), 0)
    slab = lane % 32
    place = (row == (slab % 8) * 4 + lane // 32).astype(bf16)
    place = jnp.concatenate([place, place], axis=0)
    owner = slab // 8

    def rows(i):
        return slice(BLOCK * i, BLOCK * i + BLOCK)

    for i in range(4):
        for g in range(groups):
            matrix = blocks_ref[g, i].reshape(2 * BLOCK, BLOCK)
            rest = matrix - matrix.astype(bf16).astype(f32)
            spread = mul(jnp.concatenate([matrix, rest], axis=1).astype(bf16), place)
            hold_ref[g, rows(i), :] = jnp.where(
                owner == columns_ref[g, 2 * i], spread[:BLOCK], 0.0
            ) + jnp.where(owner == columns_ref[g, 2 * i + 1], spread[BLOCK:], 0.0)
    for half, order in ((0, (0, 1, 2, 3)), (1, (3, 2, 1, 0))):
        for step, i in enumerate(order):
            if step:
                last = order[step - 1]
                coupled = min(i, last)
                for g in range(groups):
                    hold_ref[g, rows(i), :] -= three(
                        off_ref[g, half, coupled], hold_ref[g, rows(last), :]
                    )
            for g in range(groups):
                hold_ref[g, rows(i), :] = three(diag_ref[g, half, i], hold_ref[g, rows(i), :])
    for g in range(groups):
        for level in range(4):
            high, low = split(hold_ref[g, pl.ds(level, 32, stride=4), :])
            out_ref[g, rows(level), 0:LANES] = high
            out_ref[g, rows(level), LANES:] = low


def apply_kernel(in_ref, operator_ref, out_ref):
    slabs = 32
    first = lane_index((LANES, LANES)) < 64
    for r in range(8):
        parts = [in_ref[pl.ds(8 * q1 + r, slabs, stride=32), :] for q1 in range(4)]
        values = jnp.concatenate(swap_groups(parts), axis=0)
        high, low = split(values)
        wide = jnp.concatenate(
            [
                jnp.concatenate([high, low], axis=1),
                jnp.concatenate([high, jnp.zeros_like(low)], axis=1),
            ],
            axis=0,
        )
        results = []
        for g in (2 * r, 2 * r + 1):
            both = mul(operator_ref[g], wide)
            results.append(both[:, :LANES] + both[:, LANES:])
        solved = jnp.where(first, results[0], results[1])
        parts = swap_groups([solved[32 * level : 32 * level + 32] for level in range(4)])
        for q1 in range(4):
            out_ref[pl.ds(8 * q1 + r, slabs, stride=32), :] = parts[q1]


def call(kernel, shape, *operands, dtype=f32, spaces=None, scratch=(), flops=0, limit=VMEM_LIMIT):
    spaces = spaces or [pltpu.VMEM] * len(operands)
    read = sum(math.prod(o.shape) * o.dtype.itemsize for o in operands)
    return pl.pallas_call(
        kernel,
        out_shape=jax.ShapeDtypeStruct(shape, dtype),
        in_specs=[pl.BlockSpec(memory_space=space) for space in spaces],
        out_specs=pl.BlockSpec(memory_space=pltpu.VMEM),
        scratch_shapes=scratch,
        cost_estimate=pl.CostEstimate(flops=flops, bytes_accessed=read, transcendentals=0),
        compiler_params=pltpu.CompilerParams(vmem_limit_bytes=limit),
    )(*operands)


def exchange(values, axis):
    return lax.all_to_all(values, axis, split_axis=0, concat_axis=0, tiled=True)


def body(grid_field, operator_blocks, op_columns, diag_inverse, off_blocks):
    depth, lines, length = grid_field.shape
    groups = operator_blocks.shape[1]
    forward_x, backward_x = x_tables()
    forward_y, backward_y = y_tables()
    square = (BLOCK, BLOCK)
    operator = call(
        operator_kernel,
        (groups, LANES, 2 * LANES),
        op_columns.reshape(groups, 8),
        operator_blocks.reshape((groups, 4, 2) + square),
        diag_inverse.reshape((groups, 2, 4) + square),
        off_blocks.reshape((groups, 2, 3) + square),
        dtype=bf16,
        spaces=[pltpu.SMEM] + [pltpu.VMEM] * 3,
        scratch=[pltpu.VMEM((groups, LANES, LANES), f32)],
        flops=2 * 3 * groups * 22 * BLOCK * BLOCK * LANES,
    )
    x_flops = 2 * 3 * depth * lines * length * HALF
    y_flops = 2 * 3 * 4 * QUARTER * 2 * QUARTER * LANES
    values = call(
        x_forward_kernel,
        (16, lines, LANES),
        grid_field,
        *forward_x,
        spaces=[pl.ANY] * 3,
        scratch=[
            pltpu.VMEM(grid_field.shape, f32),
            pltpu.VMEM((2, HALF, HALF), bf16),
            pltpu.VMEM((2, HALF, HALF), bf16),
            pltpu.SemaphoreType.DMA((2 + depth,)),
        ],
        flops=x_flops,
        limit=56 * 1024 * 1024,
    )
    values = exchange(values, "gx").reshape(NY, LANES)
    values = call(y_forward_kernel, (32, 32, LANES), values, *forward_y, flops=y_flops)
    values = exchange(values, "gy").reshape(NY, LANES)
    values = call(
        apply_kernel, (NY, LANES), values, operator, flops=2 * 3 * groups * LANES * LANES * LANES
    )
    values = exchange(values.reshape(32, 32, LANES), "gy")
    values = call(y_backward_kernel, (NY, LANES), values, *backward_y, flops=y_flops)
    values = exchange(values.reshape(16, lines, LANES), "gx")
    return call(
        x_backward_kernel, (depth, lines, length), values, *backward_x, flops=x_flops
    )


def solution(mesh):
    placed = (
        P("gy", "gx", None),
        P("gx", "gy", None, None, None),
        P("gx", "gy", None, None),
        P("gx", "gy", None, None, None),
        P("gx", "gy", None, None, None),
    )
    return jax.shard_map(
        body, mesh=mesh, in_specs=placed, out_specs=P("gy", "gx", None), check_vma=False
    )
```

```python
import functools
import math

import jax
import jax.numpy as jnp
import ml_dtypes
import numpy as np
from jax import lax
from jax.experimental import pallas as pl
from jax.experimental.pallas import tpu as pltpu
from jax.sharding import PartitionSpec as P

NX = 512
NY = 1024
QUARTER = NY // 4
HALF = NX // 2
LANES = 128
SPAN = 16
BLOCK = 32
PART = SPAN // 2
VMEM_LIMIT = 24 * 1024 * 1024

f32 = jnp.float32
bf16 = jnp.bfloat16


def split_table(table):
    high = table.astype(ml_dtypes.bfloat16)
    low = (table - high.astype(np.float64)).astype(ml_dtypes.bfloat16)
    return high, low


def x_tables():
    parity = np.arange(2).reshape(2, 1, 1)
    x = np.arange(HALF).reshape(1, HALF, 1)
    k = 2 * np.arange(HALF // 2).reshape(1, 1, HALF // 2) + parity
    angle = (x * k % NX) * (2.0 * math.pi / NX)
    shape = (2, HALF, HALF // SPAN, PART)
    cosine = np.cos(angle).reshape(shape) / math.sqrt(NX)
    sine = np.sin(angle).reshape(shape) / math.sqrt(NX)
    forward = np.stack([cosine, -sine], axis=3)
    weight = np.where(k == 0, 1.0, 2.0).reshape(2, 1, HALF // SPAN, 1, PART)
    backward = (forward * weight).reshape(2, HALF, HALF).transpose(0, 2, 1)
    return split_table(forward.reshape(2, HALF, HALF)), split_table(backward)


def y_tables():
    residue = np.arange(4).reshape(4, 1, 1)
    row = np.arange(QUARTER).reshape(1, QUARTER, 1)
    j = np.arange(QUARTER).reshape(1, 1, QUARTER)
    angle = (row * (residue + 4 * j) % NY) * (2.0 * math.pi / NY)
    cosine = np.cos(angle) / math.sqrt(NY)
    sine = np.sin(angle) / math.sqrt(NY)
    forward = np.concatenate([cosine, sine], axis=2)
    backward = np.concatenate([cosine, -sine], axis=2)
    return split_table(forward), split_table(backward)


def slab_order(count):
    levels = count // 4
    return [
        (high * levels + z) * 2 + core
        for core in (1, 0)
        for high in (1, 0)
        for z in range(levels - 1, -1, -1)
    ]


def line_order(count):
    side = math.isqrt(count)
    along_x = [*range(0, side, 2), *range(1, side, 2)]
    along_y = [0, side - 1, *range(1, side - 1)]
    return [side * y + x for x in along_x for y in along_y]


def order_tables(order):
    count = len(order)
    lane = np.arange(4 * count)
    index = 4 * np.array(order)[lane % count] + lane // count
    row = np.arange(BLOCK).reshape(BLOCK, 1)
    place = np.tile(index % BLOCK == row, (2, 1)).astype(ml_dtypes.bfloat16)
    owner = np.broadcast_to(index // BLOCK, (BLOCK, 4 * count)).astype(np.int32)
    pick = (index.reshape(-1, 1) == lane).astype(ml_dtypes.bfloat16)
    return place, owner, pick


def split(values):
    high = values.astype(bf16)
    low = (values - high.astype(f32)).astype(bf16)
    return high, low


def mul(left, right):
    return jnp.dot(left, right, preferred_element_type=f32)


def lane_index(shape):
    return lax.broadcasted_iota(jnp.int32, shape, len(shape) - 1)


def swap_groups(parts):
    parts = list(parts)
    lane = lane_index(parts[0].shape)
    distance, reach = len(parts) // 2, LANES // 2
    while distance:
        first = (lane & reach) == 0
        for i in range(len(parts)):
            if not i & distance:
                a, b = parts[i], parts[i + distance]
                parts[i] = jnp.where(first, a, pltpu.roll(b, reach, 1))
                parts[i + distance] = jnp.where(first, pltpu.roll(a, LANES - reach, 1), b)
        distance, reach = distance // 2, reach // 2
    return parts


def turned(values):
    real = (lane_index(values.shape) & PART) == 0
    return jnp.where(real, pltpu.roll(values, LANES - PART, 1), -pltpu.roll(values, PART, 1))


def x_forward_kernel(order, grid_hbm, high_hbm, low_hbm, out_ref, grid_ref, high_ref, low_ref, sems):
    depth, lines, length = grid_ref.shape
    pairs = [(high_hbm, high_ref), (low_hbm, low_ref)]
    pairs += [(grid_hbm.at[z], grid_ref.at[z]) for z in range(depth)]
    copies = [
        pltpu.make_async_copy(source, target, sems.at[i])
        for i, (source, target) in enumerate(pairs)
    ]
    for copy in copies:
        copy.start()
    for copy in copies:
        copy.wait()
    near = grid_ref[:, :, :HALF].reshape(depth * lines, HALF)
    far = grid_ref[:, :, HALF:].reshape(depth * lines, HALF)
    sums = []
    for p, values in enumerate((near + far, near - far)):
        high, low = split(values)
        wide = mul(jnp.concatenate([high, low], axis=0), high_ref[p])
        sums.append(wide[: depth * lines] + (wide[depth * lines :] + mul(high, low_ref[p])))
    for a in range(HALF // LANES):
        columns = slice(a * LANES, (a + 1) * LANES)
        parts = [
            sums[p][z * lines : (z + 1) * lines, columns] for z in range(depth) for p in range(2)
        ]
        for b, part in enumerate(swap_groups(parts)):
            out_ref[order.index(8 * a + b)] = part


def x_backward_kernel(order, in_ref, high_ref, low_ref, out_hbm, out_ref, sems):
    depth, lines, length = out_ref.shape
    columns = [
        swap_groups([in_ref[order.index(8 * a + b)] for b in range(8)])
        for a in range(HALF // LANES)
    ]
    step = 2
    copies = []
    for z in range(0, depth, step):
        levels = range(z, z + step)
        results = []
        for p in range(2):
            rows = [
                jnp.concatenate([column[2 * level + p] for column in columns], axis=1)
                for level in levels
            ]
            high, low = split(jnp.concatenate(rows, axis=0))
            wide = mul(jnp.concatenate([high, low], axis=0), high_ref[p])
            count = step * lines
            results.append(wide[:count] + (wide[count:] + mul(high, low_ref[p])))
        near, far = results
        out_ref[z : z + step, :, :HALF] = (near + far).reshape(step, lines, HALF)
        out_ref[z : z + step, :, HALF:] = (near - far).reshape(step, lines, HALF)
        for level in levels:
            copy = pltpu.make_async_copy(out_ref.at[level], out_hbm.at[level], sems.at[level])
            copy.start()
            copies.append(copy)
    for copy in copies:
        copy.wait()


def quarter_product(values, high_table, low_table):
    both = jnp.concatenate([values, turned(values)], axis=0)
    high, low = split(both)
    wide = mul(high_table, jnp.concatenate([high, low], axis=1))
    return wide[:, :LANES] + (wide[:, LANES:] + mul(low_table, high))


def load_blocks(ref, order, r):
    block = ref.shape[0] // len(order)
    parts = [
        ref[pl.ds(block * order.index(i) + r, block // 4, stride=4), :] for i in range(len(order))
    ]
    return jnp.concatenate(parts, axis=0)


def store_blocks(ref, order, quarters):
    block = ref.shape[0] // len(order)
    for place, i in enumerate(order):
        start = block * i % QUARTER
        part = quarters[block * i // QUARTER][start : start + block]
        ref[block * place : block * place + block, :] = part


def y_kernel(sign, source, target, in_ref, high_ref, low_ref, out_ref):
    products = [
        quarter_product(load_blocks(in_ref, source, r), high_ref[r], low_ref[r])
        for r in range(4)
    ]
    a, b, c, d = products
    even_sum, even_difference = a + c, a - c
    odd_sum, odd_difference = b + d, sign * turned(b - d)
    quarters = (
        even_sum + odd_sum,
        even_difference + odd_difference,
        even_sum - odd_sum,
        even_difference - odd_difference,
    )
    store_blocks(out_ref, target, quarters)


def spread_left(matrix):
    rest = matrix - matrix.astype(bf16).astype(f32)
    return jnp.concatenate([matrix, rest, matrix], axis=1).astype(bf16)


def three(matrix, right):
    high, low = split(right)
    return mul(spread_left(matrix), jnp.concatenate([high, high, low], axis=0))


def operator_kernel(
    columns_ref, blocks_ref, diag_ref, off_ref, place_ref, owner_ref, pick_ref, out_ref, hold_ref
):
    groups = blocks_ref.shape[0]
    place = place_ref[...]
    owner = owner_ref[...]

    def rows(i):
        return slice(BLOCK * i, BLOCK * i + BLOCK)

    for i in range(4):
        for g in range(groups):
            matrix = blocks_ref[g, i].reshape(2 * BLOCK, BLOCK)
            rest = matrix - matrix.astype(bf16).astype(f32)
            spread = mul(jnp.concatenate([matrix, rest], axis=1).astype(bf16), place)
            hold_ref[g, rows(i), :] = jnp.where(
                owner == columns_ref[g, 2 * i], spread[:BLOCK], 0.0
            ) + jnp.where(owner == columns_ref[g, 2 * i + 1], spread[BLOCK:], 0.0)
    for half, order in ((0, (0, 1, 2, 3)), (1, (3, 2, 1, 0))):
        for step, i in enumerate(order):
            if step:
                last = order[step - 1]
                coupled = min(i, last)
                for g in range(groups):
                    hold_ref[g, rows(i), :] -= three(
                        off_ref[g, half, coupled], hold_ref[g, rows(last), :]
                    )
            for g in range(groups):
                hold_ref[g, rows(i), :] = three(diag_ref[g, half, i], hold_ref[g, rows(i), :])
    pick = pick_ref[...]
    for g in range(groups):
        high, low = split(hold_ref[g])
        ordered = mul(pick, jnp.concatenate([high, low], axis=1))
        out_ref[g] = ordered.astype(bf16)


def apply_kernel(in_ref, operator_ref, out_ref):
    slabs = in_ref.shape[0] // 32
    first = lane_index((LANES, LANES)) < 64
    wide = []
    for r in range(8):
        parts = [in_ref[pl.ds(4 * r + i, slabs, stride=32), :] for i in range(4)]
        high, low = split(jnp.concatenate(swap_groups(parts), axis=0))
        upper = jnp.concatenate([high, low], axis=1)
        lower = jnp.concatenate([high, jnp.zeros_like(low)], axis=1)
        wide.append(jnp.concatenate([upper, lower], axis=0))
    solved = []
    for r in range(8):
        both = mul(operator_ref[2 * r : 2 * r + 2].reshape(2 * LANES, 2 * LANES), wide[r])
        both = both[:, :LANES] + both[:, LANES:]
        solved.append(jnp.where(first, both[:LANES], both[LANES:]))
    for r in range(8):
        parts = swap_groups([solved[r][32 * level : 32 * level + 32] for level in range(4)])
        for i in range(4):
            out_ref[pl.ds(4 * r + i, slabs, stride=32), :] = parts[i]


def call(kernel, shape, *operands, dtype=f32, spaces=None, out=None, scratch=(), flops=0):
    spaces = spaces or [None] * len(operands)
    read = sum(math.prod(o.shape) * o.dtype.itemsize for o in operands)
    operands = [
        operand if space in (None, pltpu.SMEM) else pltpu.with_memory_space_constraint(operand, space)
        for space, operand in zip(spaces, operands)
    ]
    return pl.pallas_call(
        kernel,
        out_shape=jax.ShapeDtypeStruct(shape, dtype),
        in_specs=[pl.BlockSpec(memory_space=space or pltpu.VMEM) for space in spaces],
        out_specs=pl.BlockSpec(memory_space=out or pltpu.VMEM),
        scratch_shapes=scratch,
        cost_estimate=pl.CostEstimate(flops=flops, bytes_accessed=read, transcendentals=0),
        compiler_params=pltpu.CompilerParams(vmem_limit_bytes=VMEM_LIMIT),
    )(*operands)


def exchange(values, axis, order=None):
    members = None if order is None else [order]
    return lax.all_to_all(
        values, axis, split_axis=0, concat_axis=0, axis_index_groups=members, tiled=True
    )


def body(grid_field, operator_blocks, op_columns, diag_inverse, off_blocks):
    depth, lines, length = grid_field.shape
    groups = operator_blocks.shape[1]
    forward_x, backward_x = x_tables()
    forward_y, backward_y = y_tables()
    order = slab_order(32)
    line = line_order(16)
    square = (BLOCK, BLOCK)
    operator = call(
        operator_kernel,
        (groups, LANES, 2 * LANES),
        op_columns.reshape(groups, 8),
        operator_blocks.reshape((groups, 4, 2) + square),
        diag_inverse.reshape((groups, 2, 4) + square),
        off_blocks.reshape((groups, 2, 3) + square),
        *order_tables(order),
        dtype=bf16,
        spaces=[pltpu.SMEM] + [None] * 6,
        scratch=[pltpu.VMEM((groups, LANES, LANES), f32)],
        flops=2 * 3 * groups * 22 * BLOCK * BLOCK * LANES,
    )
    x_flops = 2 * 3 * depth * lines * length * HALF
    y_flops = 2 * 3 * 4 * QUARTER * 2 * QUARTER * LANES
    values = call(
        functools.partial(x_forward_kernel, line),
        (16, lines, LANES),
        grid_field,
        *forward_x,
        spaces=[pltpu.HBM] * 3,
        scratch=[
            pltpu.VMEM(grid_field.shape, f32),
            pltpu.VMEM((2, HALF, HALF), bf16),
            pltpu.VMEM((2, HALF, HALF), bf16),
            pltpu.SemaphoreType.DMA((2 + depth,)),
        ],
        flops=x_flops,
    )
    values = exchange(values, "gx", line).reshape(NY, LANES)
    values = call(
        functools.partial(y_kernel, 1.0, line, order), (NY, LANES), values, *forward_y, flops=y_flops
    )
    values = exchange(values.reshape(32, 32, LANES), "gy", order).reshape(NY, LANES)
    values = call(
        apply_kernel,
        (NY, LANES),
        values,
        operator,
        flops=2 * 3 * groups * LANES * LANES * LANES,
    )
    values = exchange(values.reshape(32, 32, LANES), "gy", order).reshape(NY, LANES)
    values = call(
        functools.partial(y_kernel, -1.0, order, line), (NY, LANES), values, *backward_y, flops=y_flops
    )
    values = exchange(values.reshape(16, lines, LANES), "gx", line)
    return call(
        functools.partial(x_backward_kernel, line),
        (depth, lines, length),
        values,
        *backward_x,
        out=pl.ANY,
        scratch=[pltpu.VMEM((depth, lines, length), f32), pltpu.SemaphoreType.DMA((depth,))],
        flops=x_flops,
    )


def solution(mesh):
    placed = (
        P("gy", "gx", None),
        P("gx", "gy", None, None, None),
        P("gx", "gy", None, None),
        P("gx", "gy", None, None, None),
        P("gx", "gy", None, None, None),
    )
    return jax.shard_map(
        body, mesh=mesh, in_specs=placed, out_specs=P("gy", "gx", None), check_vma=False
    )
```

```python
import functools
import math

import jax
import jax.numpy as jnp
import ml_dtypes
import numpy as np
from jax import lax
from jax.experimental import pallas as pl
from jax.experimental.pallas import tpu as pltpu
from jax.sharding import PartitionSpec as P

NX = 512
NY = 1024
QUARTER = NY // 4
HALF = NX // 2
LANES = 128
SPAN = 16
BLOCK = 32
PART = SPAN // 2
VMEM_LIMIT = 24 * 1024 * 1024

f32 = jnp.float32
bf16 = jnp.bfloat16


def split_table(table):
    high = table.astype(ml_dtypes.bfloat16)
    low = (table - high.astype(np.float64)).astype(ml_dtypes.bfloat16)
    return high, low


def x_tables():
    parity = np.arange(2).reshape(2, 1, 1)
    x = np.arange(HALF).reshape(1, HALF, 1)
    k = 2 * np.arange(HALF // 2).reshape(1, 1, HALF // 2) + parity
    angle = (x * k % NX) * (2.0 * math.pi / NX)
    shape = (2, HALF, HALF // SPAN, PART)
    cosine = np.cos(angle).reshape(shape) / math.sqrt(NX)
    sine = np.sin(angle).reshape(shape) / math.sqrt(NX)
    forward = np.stack([cosine, -sine], axis=3)
    weight = np.where(k == 0, 1.0, 2.0).reshape(2, 1, HALF // SPAN, 1, PART)
    backward = (forward * weight).reshape(2, HALF, HALF).transpose(0, 2, 1)
    return split_table(forward.reshape(2, HALF, HALF)), split_table(backward)


def y_tables():
    residue = np.arange(4).reshape(4, 1, 1)
    row = np.arange(QUARTER).reshape(1, QUARTER, 1)
    j = np.arange(QUARTER).reshape(1, 1, QUARTER)
    angle = (row * (residue + 4 * j) % NY) * (2.0 * math.pi / NY)
    cosine = np.cos(angle) / math.sqrt(NY)
    sine = np.sin(angle) / math.sqrt(NY)
    forward = np.concatenate([cosine, sine], axis=2)
    backward = np.concatenate([cosine, -sine], axis=2)
    return split_table(forward), split_table(backward)


def slab_order(count):
    levels = count // 4
    return [
        (high * levels + (levels - 2 - i) % levels) * 2 + core
        for high in (1, 0)
        for core in (1, 0)
        for i in range(levels)
    ]


def line_order():
    return [4 * y + x for x in (1, 3, 2, 0) for y in (2, 1, 0, 3)]


def order_tables(order):
    count = len(order)
    lane = np.arange(4 * count)
    index = 4 * np.array(order)[lane % count] + lane // count
    row = np.arange(BLOCK).reshape(BLOCK, 1)
    place = np.tile(index % BLOCK == row, (2, 1)).astype(ml_dtypes.bfloat16)
    owner = np.broadcast_to(index // BLOCK, (BLOCK, 4 * count)).astype(np.int32)
    pick = (index.reshape(-1, 1) == lane).astype(ml_dtypes.bfloat16)
    return place, owner, pick


def split(values):
    high = values.astype(bf16)
    low = (values - high.astype(f32)).astype(bf16)
    return high, low


def mul(left, right):
    return jnp.dot(left, right, preferred_element_type=f32)


def lane_index(shape):
    return lax.broadcasted_iota(jnp.int32, shape, len(shape) - 1)


def swap_groups(parts):
    parts = list(parts)
    lane = lane_index(parts[0].shape)
    distance, reach = len(parts) // 2, LANES // 2
    while distance:
        first = (lane & reach) == 0
        for i in range(len(parts)):
            if not i & distance:
                a, b = parts[i], parts[i + distance]
                parts[i] = jnp.where(first, a, pltpu.roll(b, reach, 1))
                parts[i + distance] = jnp.where(first, pltpu.roll(a, LANES - reach, 1), b)
        distance, reach = distance // 2, reach // 2
    return parts


def turned(values):
    real = (lane_index(values.shape) & PART) == 0
    return jnp.where(real, pltpu.roll(values, LANES - PART, 1), -pltpu.roll(values, PART, 1))


def x_forward_kernel(order, grid_hbm, high_hbm, low_hbm, out_ref, grid_ref, high_ref, low_ref, sems):
    depth, lines, length = grid_ref.shape
    levels = [(grid_hbm.at[z], grid_ref.at[z]) for z in range(depth)]
    half = depth // 2
    pairs = [(high_hbm, high_ref), *levels, (low_hbm, low_ref)]
    copies = [
        pltpu.make_async_copy(source, target, sems.at[i])
        for i, (source, target) in enumerate(pairs)
    ]
    for copy in copies:
        copy.start()
    rows = lines * half
    sums = [[], []]
    for part in range(2):
        for copy in copies[1:][part * half : (part + 1) * half] if part else copies[: 1 + half]:
            copy.wait()
        window = slice(part * half, (part + 1) * half)
        near = grid_ref[window, :, :HALF].reshape(rows, HALF)
        far = grid_ref[window, :, HALF:].reshape(rows, HALF)
        for p, values in enumerate((near + far, near - far)):
            high, low = split(values)
            wide = mul(jnp.concatenate([high, low], axis=0), high_ref[p])
            sums[p].append((high, wide[:rows] + wide[rows:]))
    copies[-1].wait()
    sums = [
        jnp.concatenate([total + mul(high, low_ref[p]) for high, total in sums[p]], axis=0)
        for p in range(2)
    ]
    for a in range(HALF // LANES):
        columns = slice(a * LANES, (a + 1) * LANES)
        parts = [
            sums[p][z * lines : (z + 1) * lines, columns] for z in range(depth) for p in range(2)
        ]
        for b, part in enumerate(swap_groups(parts)):
            out_ref[order.index(8 * a + b)] = part


def x_backward_kernel(order, in_ref, high_ref, low_ref, out_hbm, out_ref, sems):
    depth, lines, length = out_ref.shape
    columns = [
        swap_groups([in_ref[order.index(8 * a + b)] for b in range(8)])
        for a in range(HALF // LANES)
    ]
    step = 2
    copies = []
    for z in range(0, depth, step):
        levels = range(z, z + step)
        results = []
        for p in range(2):
            rows = [
                jnp.concatenate([column[2 * level + p] for column in columns], axis=1)
                for level in levels
            ]
            high, low = split(jnp.concatenate(rows, axis=0))
            wide = mul(jnp.concatenate([high, low], axis=0), high_ref[p])
            count = step * lines
            results.append(wide[:count] + (wide[count:] + mul(high, low_ref[p])))
        near, far = results
        out_ref[z : z + step, :, :HALF] = (near + far).reshape(step, lines, HALF)
        out_ref[z : z + step, :, HALF:] = (near - far).reshape(step, lines, HALF)
        for level in levels:
            copy = pltpu.make_async_copy(out_ref.at[level], out_hbm.at[level], sems.at[level])
            copy.start()
            copies.append(copy)
    for copy in copies:
        copy.wait()


def quarter_product(values, high_table, low_table):
    both = jnp.concatenate([values, turned(values)], axis=0)
    high, low = split(both)
    wide = mul(high_table, jnp.concatenate([high, low], axis=1))
    return wide[:, :LANES] + (wide[:, LANES:] + mul(low_table, high))


def load_blocks(ref, order, r):
    block = ref.shape[0] // len(order)
    parts = [
        ref[pl.ds(block * order.index(i) + r, block // 4, stride=4), :] for i in range(len(order))
    ]
    return jnp.concatenate(parts, axis=0)


def store_blocks(ref, order, quarters):
    block = ref.shape[0] // len(order)
    for place, i in enumerate(order):
        start = block * i % QUARTER
        part = quarters[block * i // QUARTER][start : start + block]
        ref[block * place : block * place + block, :] = part


def y_kernel(sign, source, target, in_ref, high_ref, low_ref, out_ref):
    products = [
        quarter_product(load_blocks(in_ref, source, r), high_ref[r], low_ref[r])
        for r in range(4)
    ]
    a, b, c, d = products
    even_sum, even_difference = a + c, a - c
    odd_sum, odd_difference = b + d, sign * turned(b - d)
    quarters = (
        even_sum + odd_sum,
        even_difference + odd_difference,
        even_sum - odd_sum,
        even_difference - odd_difference,
    )
    store_blocks(out_ref, target, quarters)


def spread_left(matrix):
    rest = matrix - matrix.astype(bf16).astype(f32)
    return jnp.concatenate([matrix, rest, matrix], axis=1).astype(bf16)


def three(matrix, right):
    high, low = split(right)
    return mul(spread_left(matrix), jnp.concatenate([high, high, low], axis=0))


def operator_kernel(
    columns_ref, blocks_ref, diag_ref, off_ref, place_ref, owner_ref, pick_ref, out_ref, hold_ref
):
    groups = blocks_ref.shape[0]
    place = place_ref[...]
    owner = owner_ref[...]

    def rows(i):
        return slice(BLOCK * i, BLOCK * i + BLOCK)

    for i in range(4):
        for g in range(groups):
            matrix = blocks_ref[g, i].reshape(2 * BLOCK, BLOCK)
            rest = matrix - matrix.astype(bf16).astype(f32)
            spread = mul(jnp.concatenate([matrix, rest], axis=1).astype(bf16), place)
            hold_ref[g, rows(i), :] = jnp.where(
                owner == columns_ref[g, 2 * i], spread[:BLOCK], 0.0
            ) + jnp.where(owner == columns_ref[g, 2 * i + 1], spread[BLOCK:], 0.0)
    for half, order in ((0, (0, 1, 2, 3)), (1, (3, 2, 1, 0))):
        for step, i in enumerate(order):
            if step:
                last = order[step - 1]
                coupled = min(i, last)
                for g in range(groups):
                    hold_ref[g, rows(i), :] -= three(
                        off_ref[g, half, coupled], hold_ref[g, rows(last), :]
                    )
            for g in range(groups):
                hold_ref[g, rows(i), :] = three(diag_ref[g, half, i], hold_ref[g, rows(i), :])
    pick = pick_ref[...]
    for g in range(groups):
        high, low = split(hold_ref[g])
        ordered = mul(pick, jnp.concatenate([high, low], axis=1))
        out_ref[g] = ordered.astype(bf16)


def apply_kernel(in_ref, operator_ref, out_ref):
    slabs = in_ref.shape[0] // 32
    first = lane_index((LANES, LANES)) < 64
    wide = []
    for r in range(8):
        parts = [in_ref[pl.ds(4 * r + i, slabs, stride=32), :] for i in range(4)]
        high, low = split(jnp.concatenate(swap_groups(parts), axis=0))
        upper = jnp.concatenate([high, low], axis=1)
        lower = jnp.concatenate([high, jnp.zeros_like(low)], axis=1)
        wide.append(jnp.concatenate([upper, lower], axis=0))
    solved = []
    for r in range(8):
        both = mul(operator_ref[2 * r : 2 * r + 2].reshape(2 * LANES, 2 * LANES), wide[r])
        both = both[:, :LANES] + both[:, LANES:]
        solved.append(jnp.where(first, both[:LANES], both[LANES:]))
    for r in range(8):
        parts = swap_groups([solved[r][32 * level : 32 * level + 32] for level in range(4)])
        for i in range(4):
            out_ref[pl.ds(4 * r + i, slabs, stride=32), :] = parts[i]


def call(kernel, shape, *operands, dtype=f32, spaces=None, out=None, scratch=(), flops=0):
    spaces = spaces or [None] * len(operands)
    read = sum(math.prod(o.shape) * o.dtype.itemsize for o in operands)
    operands = [
        operand if space in (None, pltpu.SMEM) else pltpu.with_memory_space_constraint(operand, space)
        for space, operand in zip(spaces, operands)
    ]
    return pl.pallas_call(
        kernel,
        out_shape=jax.ShapeDtypeStruct(shape, dtype),
        in_specs=[pl.BlockSpec(memory_space=space or pltpu.VMEM) for space in spaces],
        out_specs=pl.BlockSpec(memory_space=out or pltpu.VMEM),
        scratch_shapes=scratch,
        cost_estimate=pl.CostEstimate(flops=flops, bytes_accessed=read, transcendentals=0),
        compiler_params=pltpu.CompilerParams(vmem_limit_bytes=VMEM_LIMIT),
    )(*operands)


def exchange(values, axis, order=None):
    members = None if order is None else [order]
    return lax.all_to_all(
        values, axis, split_axis=0, concat_axis=0, axis_index_groups=members, tiled=True
    )


def body(grid_field, operator_blocks, op_columns, diag_inverse, off_blocks):
    depth, lines, length = grid_field.shape
    groups = operator_blocks.shape[1]
    forward_x, backward_x = x_tables()
    forward_y, backward_y = y_tables()
    order = slab_order(32)
    line = line_order()
    square = (BLOCK, BLOCK)
    operator = call(
        operator_kernel,
        (groups, LANES, 2 * LANES),
        op_columns.reshape(groups, 8),
        operator_blocks.reshape((groups, 4, 2) + square),
        diag_inverse.reshape((groups, 2, 4) + square),
        off_blocks.reshape((groups, 2, 3) + square),
        *order_tables(order),
        dtype=bf16,
        spaces=[pltpu.SMEM] + [None] * 6,
        scratch=[pltpu.VMEM((groups, LANES, LANES), f32)],
        flops=2 * 3 * groups * 22 * BLOCK * BLOCK * LANES,
    )
    x_flops = 2 * 3 * depth * lines * length * HALF
    y_flops = 2 * 3 * 4 * QUARTER * 2 * QUARTER * LANES
    values = call(
        functools.partial(x_forward_kernel, line),
        (16, lines, LANES),
        grid_field,
        *forward_x,
        spaces=[pltpu.HBM] * 3,
        scratch=[
            pltpu.VMEM(grid_field.shape, f32),
            pltpu.VMEM((2, HALF, HALF), bf16),
            pltpu.VMEM((2, HALF, HALF), bf16),
            pltpu.SemaphoreType.DMA((2 + depth,)),
        ],
        flops=x_flops,
    )
    values = exchange(values, "gx", line).reshape(NY, LANES)
    values = call(
        functools.partial(y_kernel, 1.0, line, order), (NY, LANES), values, *forward_y, flops=y_flops
    )
    values = exchange(values.reshape(32, 32, LANES), "gy", order).reshape(NY, LANES)
    values = call(
        apply_kernel,
        (NY, LANES),
        values,
        operator,
        flops=2 * 3 * groups * LANES * LANES * LANES,
    )
    values = exchange(values.reshape(32, 32, LANES), "gy", order).reshape(NY, LANES)
    values = call(
        functools.partial(y_kernel, -1.0, order, line), (NY, LANES), values, *backward_y, flops=y_flops
    )
    values = exchange(values.reshape(16, lines, LANES), "gx", line)
    return call(
        functools.partial(x_backward_kernel, line),
        (depth, lines, length),
        values,
        *backward_x,
        out=pl.ANY,
        scratch=[pltpu.VMEM((depth, lines, length), f32), pltpu.SemaphoreType.DMA((depth,))],
        flops=x_flops,
    )


def solution(mesh):
    placed = (
        P("gy", "gx", None),
        P("gx", "gy", None, None, None),
        P("gx", "gy", None, None),
        P("gx", "gy", None, None, None),
        P("gx", "gy", None, None, None),
    )
    return jax.shard_map(
        body, mesh=mesh, in_specs=placed, out_specs=P("gy", "gx", None), check_vma=False
    )
```

```python
import functools
import math

import jax
import jax.numpy as jnp
import ml_dtypes
import numpy as np
from jax import lax
from jax.experimental import pallas as pl
from jax.experimental.pallas import tpu as pltpu
from jax.sharding import PartitionSpec as P

NX = 512
NY = 1024
QUARTER = NY // 4
HALF = NX // 2
LANES = 128
SPAN = 16
BLOCK = 32
PART = SPAN // 2
VMEM_LIMIT = 24 * 1024 * 1024

f32 = jnp.float32
bf16 = jnp.bfloat16


def split_table(table):
    high = table.astype(ml_dtypes.bfloat16)
    low = (table - high.astype(np.float64)).astype(ml_dtypes.bfloat16)
    return high, low


def x_tables():
    parity = np.arange(2).reshape(2, 1, 1)
    x = np.arange(HALF).reshape(1, HALF, 1)
    k = 2 * np.arange(HALF // 2).reshape(1, 1, HALF // 2) + parity
    angle = (x * k % NX) * (2.0 * math.pi / NX)
    shape = (2, HALF, HALF // SPAN, PART)
    cosine = np.cos(angle).reshape(shape) / math.sqrt(NX)
    sine = np.sin(angle).reshape(shape) / math.sqrt(NX)
    forward = np.stack([cosine, -sine], axis=3)
    weight = np.where(k == 0, 1.0, 2.0).reshape(2, 1, HALF // SPAN, 1, PART)
    backward = (forward * weight).reshape(2, HALF, HALF).transpose(0, 2, 1)
    return split_table(forward.reshape(2, HALF, HALF)), split_table(backward)


def y_tables():
    residue = np.arange(4).reshape(4, 1, 1)
    row = np.arange(QUARTER).reshape(1, QUARTER, 1)
    j = np.arange(QUARTER).reshape(1, 1, QUARTER)
    angle = (row * (residue + 4 * j) % NY) * (2.0 * math.pi / NY)
    cosine = np.cos(angle) / math.sqrt(NY)
    sine = np.sin(angle) / math.sqrt(NY)
    forward = np.concatenate([cosine, sine], axis=2)
    backward = np.concatenate([cosine, -sine], axis=2)
    return split_table(forward), split_table(backward)


def slab_order(highs, cores, levels):
    return [(8 * high + z) * 2 + core for high in highs for core in cores for z in levels]


def line_order(along_x, along_y):
    return [4 * y + x for x in along_x for y in along_y]


SLABS_THERE = slab_order((1, 0), (1, 0), (7, 6, 5, 4, 3, 2, 1, 0))
SLABS_BACK = slab_order((1, 0), (1, 0), (6, 5, 4, 3, 2, 1, 0, 7))
LINES_THERE = line_order((2, 1, 3, 0), (1, 2, 3, 0))
LINES_BACK = line_order((1, 3, 2, 0), (2, 1, 0, 3))


def operator_tables(there, back):
    def levels(order):
        lane = np.arange(4 * len(order))
        return 4 * np.array(order)[lane % len(order)] + lane // len(order)

    column, line = levels(there), levels(back)
    row = np.arange(BLOCK).reshape(BLOCK, 1)
    place = np.tile(column % BLOCK == row, (2, 1)).astype(ml_dtypes.bfloat16)
    owner = np.broadcast_to(column // BLOCK, (BLOCK, len(column))).astype(np.int32)
    pick = (line.reshape(-1, 1) == np.arange(len(line))).astype(ml_dtypes.bfloat16)
    return place, owner, pick


def split(values):
    high = values.astype(bf16)
    low = (values - high.astype(f32)).astype(bf16)
    return high, low


def mul(left, right):
    return jnp.dot(left, right, preferred_element_type=f32)


def lane_index(shape):
    return lax.broadcasted_iota(jnp.int32, shape, len(shape) - 1)


def swap_groups(parts):
    parts = list(parts)
    lane = lane_index(parts[0].shape)
    distance, reach = len(parts) // 2, LANES // 2
    while distance:
        first = (lane & reach) == 0
        for i in range(len(parts)):
            if not i & distance:
                a, b = parts[i], parts[i + distance]
                parts[i] = jnp.where(first, a, pltpu.roll(b, reach, 1))
                parts[i + distance] = jnp.where(first, pltpu.roll(a, LANES - reach, 1), b)
        distance, reach = distance // 2, reach // 2
    return parts


def turned(values):
    real = (lane_index(values.shape) & PART) == 0
    return jnp.where(real, pltpu.roll(values, LANES - PART, 1), -pltpu.roll(values, PART, 1))


def x_forward_kernel(order, grid_hbm, high_hbm, low_hbm, out_ref, grid_ref, high_ref, low_ref, sems):
    depth, lines, length = grid_ref.shape
    levels = [(grid_hbm.at[z], grid_ref.at[z]) for z in range(depth)]
    half = depth // 2
    pairs = [(high_hbm, high_ref), *levels, (low_hbm, low_ref)]
    copies = [
        pltpu.make_async_copy(source, target, sems.at[i])
        for i, (source, target) in enumerate(pairs)
    ]
    for copy in copies:
        copy.start()
    rows = lines * half
    sums = [[], []]
    for part in range(2):
        for copy in copies[1:][part * half : (part + 1) * half] if part else copies[: 1 + half]:
            copy.wait()
        window = slice(part * half, (part + 1) * half)
        near = grid_ref[window, :, :HALF].reshape(rows, HALF)
        far = grid_ref[window, :, HALF:].reshape(rows, HALF)
        for p, values in enumerate((near + far, near - far)):
            high, low = split(values)
            wide = mul(jnp.concatenate([high, low], axis=0), high_ref[p])
            sums[p].append((high, wide[:rows] + wide[rows:]))
    copies[-1].wait()
    sums = [
        jnp.concatenate([total + mul(high, low_ref[p]) for high, total in sums[p]], axis=0)
        for p in range(2)
    ]
    for a in range(HALF // LANES):
        columns = slice(a * LANES, (a + 1) * LANES)
        parts = [
            sums[p][z * lines : (z + 1) * lines, columns] for z in range(depth) for p in range(2)
        ]
        for b, part in enumerate(swap_groups(parts)):
            out_ref[order.index(8 * a + b)] = part


def x_backward_kernel(order, in_ref, high_ref, low_ref, out_hbm, out_ref, sems):
    depth, lines, length = out_ref.shape
    columns = [
        swap_groups([in_ref[order.index(8 * a + b)] for b in range(8)])
        for a in range(HALF // LANES)
    ]
    step = 2
    copies = []
    for z in range(0, depth, step):
        levels = range(z, z + step)
        results = []
        for p in range(2):
            rows = [
                jnp.concatenate([column[2 * level + p] for column in columns], axis=1)
                for level in levels
            ]
            high, low = split(jnp.concatenate(rows, axis=0))
            wide = mul(jnp.concatenate([high, low], axis=0), high_ref[p])
            count = step * lines
            results.append(wide[:count] + (wide[count:] + mul(high, low_ref[p])))
        near, far = results
        out_ref[z : z + step, :, :HALF] = (near + far).reshape(step, lines, HALF)
        out_ref[z : z + step, :, HALF:] = (near - far).reshape(step, lines, HALF)
        for level in levels:
            copy = pltpu.make_async_copy(out_ref.at[level], out_hbm.at[level], sems.at[level])
            copy.start()
            copies.append(copy)
    for copy in copies:
        copy.wait()


def quarter_product(values, high_table, low_table):
    both = jnp.concatenate([values, turned(values)], axis=0)
    high, low = split(both)
    wide = mul(high_table, jnp.concatenate([high, low], axis=1))
    return wide[:, :LANES] + (wide[:, LANES:] + mul(low_table, high))


def load_blocks(ref, order, r):
    block = ref.shape[0] // len(order)
    parts = [
        ref[pl.ds(block * order.index(i) + r, block // 4, stride=4), :] for i in range(len(order))
    ]
    return jnp.concatenate(parts, axis=0)


def store_blocks(ref, order, quarters):
    block = ref.shape[0] // len(order)
    for place, i in enumerate(order):
        start = block * i % QUARTER
        part = quarters[block * i // QUARTER][start : start + block]
        ref[block * place : block * place + block, :] = part


def y_kernel(sign, source, target, in_ref, high_ref, low_ref, out_ref):
    products = [
        quarter_product(load_blocks(in_ref, source, r), high_ref[r], low_ref[r])
        for r in range(4)
    ]
    a, b, c, d = products
    even_sum, even_difference = a + c, a - c
    odd_sum, odd_difference = b + d, sign * turned(b - d)
    quarters = (
        even_sum + odd_sum,
        even_difference + odd_difference,
        even_sum - odd_sum,
        even_difference - odd_difference,
    )
    store_blocks(out_ref, target, quarters)


def spread_left(matrix):
    rest = matrix - matrix.astype(bf16).astype(f32)
    return jnp.concatenate([matrix, rest, matrix], axis=1).astype(bf16)


def three(matrix, right):
    high, low = split(right)
    return mul(spread_left(matrix), jnp.concatenate([high, high, low], axis=0))


def operator_kernel(
    columns_ref, blocks_ref, diag_ref, off_ref, place_ref, owner_ref, pick_ref, out_ref, hold_ref
):
    groups = blocks_ref.shape[0]
    place = place_ref[...]
    owner = owner_ref[...]

    def rows(i):
        return slice(BLOCK * i, BLOCK * i + BLOCK)

    for i in range(4):
        for g in range(groups):
            matrix = blocks_ref[g, i].reshape(2 * BLOCK, BLOCK)
            rest = matrix - matrix.astype(bf16).astype(f32)
            spread = mul(jnp.concatenate([matrix, rest], axis=1).astype(bf16), place)
            hold_ref[g, rows(i), :] = jnp.where(
                owner == columns_ref[g, 2 * i], spread[:BLOCK], 0.0
            ) + jnp.where(owner == columns_ref[g, 2 * i + 1], spread[BLOCK:], 0.0)
    for half, order in ((0, (0, 1, 2, 3)), (1, (3, 2, 1, 0))):
        for step, i in enumerate(order):
            if step:
                last = order[step - 1]
                coupled = min(i, last)
                for g in range(groups):
                    hold_ref[g, rows(i), :] -= three(
                        off_ref[g, half, coupled], hold_ref[g, rows(last), :]
                    )
            for g in range(groups):
                hold_ref[g, rows(i), :] = three(diag_ref[g, half, i], hold_ref[g, rows(i), :])
    pick = pick_ref[...]
    for g in range(groups):
        high, low = split(hold_ref[g])
        ordered = mul(pick, jnp.concatenate([high, low], axis=1))
        out_ref[g] = ordered.astype(bf16)


def apply_kernel(in_ref, operator_ref, out_ref):
    slabs = in_ref.shape[0] // 32
    first = lane_index((LANES, LANES)) < 64
    wide = []
    for r in range(8):
        parts = [in_ref[pl.ds(4 * r + i, slabs, stride=32), :] for i in range(4)]
        high, low = split(jnp.concatenate(swap_groups(parts), axis=0))
        upper = jnp.concatenate([high, low], axis=1)
        lower = jnp.concatenate([high, jnp.zeros_like(low)], axis=1)
        wide.append(jnp.concatenate([upper, lower], axis=0))
    solved = []
    for r in range(8):
        both = mul(operator_ref[2 * r : 2 * r + 2].reshape(2 * LANES, 2 * LANES), wide[r])
        both = both[:, :LANES] + both[:, LANES:]
        solved.append(jnp.where(first, both[:LANES], both[LANES:]))
    for r in range(8):
        parts = swap_groups([solved[r][32 * level : 32 * level + 32] for level in range(4)])
        for i in range(4):
            out_ref[pl.ds(4 * r + i, slabs, stride=32), :] = parts[i]


def call(kernel, shape, *operands, dtype=f32, spaces=None, out=None, scratch=(), flops=0):
    spaces = spaces or [None] * len(operands)
    read = sum(math.prod(o.shape) * o.dtype.itemsize for o in operands)
    operands = [
        operand if space in (None, pltpu.SMEM) else pltpu.with_memory_space_constraint(operand, space)
        for space, operand in zip(spaces, operands)
    ]
    return pl.pallas_call(
        kernel,
        out_shape=jax.ShapeDtypeStruct(shape, dtype),
        in_specs=[pl.BlockSpec(memory_space=space or pltpu.VMEM) for space in spaces],
        out_specs=pl.BlockSpec(memory_space=out or pltpu.VMEM),
        scratch_shapes=scratch,
        cost_estimate=pl.CostEstimate(flops=flops, bytes_accessed=read, transcendentals=0),
        compiler_params=pltpu.CompilerParams(vmem_limit_bytes=VMEM_LIMIT),
    )(*operands)


def exchange(values, axis, order=None):
    members = None if order is None else [order]
    return lax.all_to_all(
        values, axis, split_axis=0, concat_axis=0, axis_index_groups=members, tiled=True
    )


def body(grid_field, operator_blocks, op_columns, diag_inverse, off_blocks):
    depth, lines, length = grid_field.shape
    groups = operator_blocks.shape[1]
    forward_x, backward_x = x_tables()
    forward_y, backward_y = y_tables()
    square = (BLOCK, BLOCK)
    operator = call(
        operator_kernel,
        (groups, LANES, 2 * LANES),
        op_columns.reshape(groups, 8),
        operator_blocks.reshape((groups, 4, 2) + square),
        diag_inverse.reshape((groups, 2, 4) + square),
        off_blocks.reshape((groups, 2, 3) + square),
        *operator_tables(SLABS_THERE, SLABS_BACK),
        dtype=bf16,
        spaces=[pltpu.SMEM] + [None] * 6,
        scratch=[pltpu.VMEM((groups, LANES, LANES), f32)],
        flops=2 * 3 * groups * 22 * BLOCK * BLOCK * LANES,
    )
    x_flops = 2 * 3 * depth * lines * length * HALF
    y_flops = 2 * 3 * 4 * QUARTER * 2 * QUARTER * LANES
    values = call(
        functools.partial(x_forward_kernel, LINES_THERE),
        (16, lines, LANES),
        grid_field,
        *forward_x,
        spaces=[pltpu.HBM] * 3,
        scratch=[
            pltpu.VMEM(grid_field.shape, f32),
            pltpu.VMEM((2, HALF, HALF), bf16),
            pltpu.VMEM((2, HALF, HALF), bf16),
            pltpu.SemaphoreType.DMA((2 + depth,)),
        ],
        flops=x_flops,
    )
    values = exchange(values, "gx", LINES_THERE).reshape(NY, LANES)
    values = call(
        functools.partial(y_kernel, 1.0, LINES_THERE, SLABS_THERE), (NY, LANES), values, *forward_y, flops=y_flops
    )
    values = exchange(values.reshape(32, 32, LANES), "gy", SLABS_THERE).reshape(NY, LANES)
    values = call(
        apply_kernel,
        (NY, LANES),
        values,
        operator,
        flops=2 * 3 * groups * LANES * LANES * LANES,
    )
    values = exchange(values.reshape(32, 32, LANES), "gy", SLABS_BACK).reshape(NY, LANES)
    values = call(
        functools.partial(y_kernel, -1.0, SLABS_BACK, LINES_BACK), (NY, LANES), values, *backward_y, flops=y_flops
    )
    values = exchange(values.reshape(16, lines, LANES), "gx", LINES_BACK)
    return call(
        functools.partial(x_backward_kernel, LINES_BACK),
        (depth, lines, length),
        values,
        *backward_x,
        out=pl.ANY,
        scratch=[pltpu.VMEM((depth, lines, length), f32), pltpu.SemaphoreType.DMA((depth,))],
        flops=x_flops,
    )


def solution(mesh):
    placed = (
        P("gy", "gx", None),
        P("gx", "gy", None, None, None),
        P("gx", "gy", None, None),
        P("gx", "gy", None, None, None),
        P("gx", "gy", None, None, None),
    )
    return jax.shard_map(
        body, mesh=mesh, in_specs=placed, out_specs=P("gy", "gx", None), check_vma=False
    )
```

```python
import functools
import math

import jax
import jax.numpy as jnp
import ml_dtypes
import numpy as np
from jax import lax
from jax.experimental import pallas as pl
from jax.experimental.pallas import tpu as pltpu
from jax.sharding import PartitionSpec as P

NX = 512
NY = 1024
QUARTER = NY // 4
HALF = NX // 2
LANES = 128
SPAN = 16
BLOCK = 32
PART = SPAN // 2
VMEM_LIMIT = 24 * 1024 * 1024

f32 = jnp.float32
bf16 = jnp.bfloat16


def split_table(table):
    high = table.astype(ml_dtypes.bfloat16)
    low = (table - high.astype(np.float64)).astype(ml_dtypes.bfloat16)
    return high, low


def x_tables():
    parity = np.arange(2).reshape(2, 1, 1)
    x = np.arange(HALF).reshape(1, HALF, 1)
    k = 2 * np.arange(HALF // 2).reshape(1, 1, HALF // 2) + parity
    angle = (x * k % NX) * (2.0 * math.pi / NX)
    shape = (2, HALF, HALF // SPAN, PART)
    cosine = np.cos(angle).reshape(shape) / math.sqrt(NX)
    sine = np.sin(angle).reshape(shape) / math.sqrt(NX)
    forward = np.stack([cosine, -sine], axis=3)
    weight = np.where(k == 0, 1.0, 2.0).reshape(2, 1, HALF // SPAN, 1, PART)
    backward = (forward * weight).reshape(2, HALF, HALF).transpose(0, 2, 1)
    return split_table(forward.reshape(2, HALF, HALF)), split_table(backward)


def y_tables():
    residue = np.arange(4).reshape(4, 1, 1)
    row = np.arange(QUARTER).reshape(1, QUARTER, 1)
    j = np.arange(QUARTER).reshape(1, 1, QUARTER)
    angle = (row * (residue + 4 * j) % NY) * (2.0 * math.pi / NY)
    cosine = np.cos(angle) / math.sqrt(NY)
    sine = np.sin(angle) / math.sqrt(NY)
    forward = np.concatenate([cosine, sine], axis=2)
    backward = np.concatenate([cosine, -sine], axis=2)
    return split_table(forward), split_table(backward)


def slab_order(highs, cores, levels):
    return [(8 * high + z) * 2 + core for high in highs for core in cores for z in levels]


def line_order(along_x, along_y):
    return [4 * y + x for x in along_x for y in along_y]


SLABS_THERE = slab_order((1, 0), (1, 0), (7, 6, 5, 4, 3, 2, 1, 0))
SLABS_BACK = slab_order((1, 0), (1, 0), (6, 5, 4, 3, 2, 1, 0, 7))
LINES_THERE = line_order((2, 1, 3, 0), (1, 2, 3, 0))
LINES_BACK = line_order((2, 1, 3, 0), (1, 2, 3, 0))


def operator_tables(there, back):
    def levels(order):
        lane = np.arange(4 * len(order))
        return 4 * np.array(order)[lane % len(order)] + lane // len(order)

    column, line = levels(there), levels(back)
    row = np.arange(BLOCK).reshape(BLOCK, 1)
    place = np.tile(column % BLOCK == row, (2, 1)).astype(ml_dtypes.bfloat16)
    owner = np.broadcast_to(column // BLOCK, (BLOCK, len(column))).astype(np.int32)
    pick = (line.reshape(-1, 1) == np.arange(len(line))).astype(ml_dtypes.bfloat16)
    return place, owner, pick


def split(values):
    high = values.astype(bf16)
    low = (values - high.astype(f32)).astype(bf16)
    return high, low


def mul(left, right):
    return jnp.dot(left, right, preferred_element_type=f32)


def lane_index(shape):
    return lax.broadcasted_iota(jnp.int32, shape, len(shape) - 1)


def swap_groups(parts):
    parts = list(parts)
    lane = lane_index(parts[0].shape)
    distance, reach = len(parts) // 2, LANES // 2
    while distance:
        first = (lane & reach) == 0
        for i in range(len(parts)):
            if not i & distance:
                a, b = parts[i], parts[i + distance]
                parts[i] = jnp.where(first, a, pltpu.roll(b, reach, 1))
                parts[i + distance] = jnp.where(first, pltpu.roll(a, LANES - reach, 1), b)
        distance, reach = distance // 2, reach // 2
    return parts


def turned(values):
    real = (lane_index(values.shape) & PART) == 0
    return jnp.where(real, pltpu.roll(values, LANES - PART, 1), -pltpu.roll(values, PART, 1))


def x_forward_kernel(order, grid_hbm, high_hbm, low_hbm, out_ref, grid_ref, high_ref, low_ref, sems):
    depth, lines, length = grid_ref.shape
    levels = [(grid_hbm.at[z], grid_ref.at[z]) for z in range(depth)]
    half = depth // 2
    pairs = [(high_hbm, high_ref), *levels, (low_hbm, low_ref)]
    copies = [
        pltpu.make_async_copy(source, target, sems.at[i])
        for i, (source, target) in enumerate(pairs)
    ]
    for copy in copies:
        copy.start()
    rows = lines * half
    sums = [[], []]
    for part in range(2):
        for copy in copies[1:][part * half : (part + 1) * half] if part else copies[: 1 + half]:
            copy.wait()
        window = slice(part * half, (part + 1) * half)
        near = grid_ref[window, :, :HALF].reshape(rows, HALF)
        far = grid_ref[window, :, HALF:].reshape(rows, HALF)
        for p, values in enumerate((near + far, near - far)):
            high, low = split(values)
            wide = mul(jnp.concatenate([high, low], axis=0), high_ref[p])
            sums[p].append((high, wide[:rows] + wide[rows:]))
    copies[-1].wait()
    sums = [
        jnp.concatenate([total + mul(high, low_ref[p]) for high, total in sums[p]], axis=0)
        for p in range(2)
    ]
    for a in range(HALF // LANES):
        columns = slice(a * LANES, (a + 1) * LANES)
        parts = [
            sums[p][z * lines : (z + 1) * lines, columns] for z in range(depth) for p in range(2)
        ]
        for b, part in enumerate(swap_groups(parts)):
            out_ref[order.index(8 * a + b)] = part


def x_backward_kernel(order, in_ref, high_ref, low_ref, out_hbm, out_ref, sems):
    depth, lines, length = out_ref.shape
    columns = [
        swap_groups([in_ref[order.index(8 * a + b)] for b in range(8)])
        for a in range(HALF // LANES)
    ]
    step = 2
    copies = []
    for z in range(0, depth, step):
        levels = range(z, z + step)
        results = []
        for p in range(2):
            rows = [
                jnp.concatenate([column[2 * level + p] for column in columns], axis=1)
                for level in levels
            ]
            high, low = split(jnp.concatenate(rows, axis=0))
            wide = mul(jnp.concatenate([high, low], axis=0), high_ref[p])
            count = step * lines
            results.append(wide[:count] + (wide[count:] + mul(high, low_ref[p])))
        near, far = results
        out_ref[z : z + step, :, :HALF] = (near + far).reshape(step, lines, HALF)
        out_ref[z : z + step, :, HALF:] = (near - far).reshape(step, lines, HALF)
        for level in levels:
            copy = pltpu.make_async_copy(out_ref.at[level], out_hbm.at[level], sems.at[level])
            copy.start()
            copies.append(copy)
    for copy in copies:
        copy.wait()


def quarter_product(values, high_table, low_table):
    both = jnp.concatenate([values, turned(values)], axis=0)
    high, low = split(both)
    wide = mul(high_table, jnp.concatenate([high, low], axis=1))
    return wide[:, :LANES] + (wide[:, LANES:] + mul(low_table, high))


def load_blocks(ref, order, r):
    block = ref.shape[0] // len(order)
    parts = [
        ref[pl.ds(block * order.index(i) + r, block // 4, stride=4), :] for i in range(len(order))
    ]
    return jnp.concatenate(parts, axis=0)


def store_blocks(ref, order, quarters):
    block = ref.shape[0] // len(order)
    for place, i in enumerate(order):
        start = block * i % QUARTER
        part = quarters[block * i // QUARTER][start : start + block]
        ref[block * place : block * place + block, :] = part


def y_kernel(sign, source, target, in_ref, high_ref, low_ref, out_ref):
    products = [
        quarter_product(load_blocks(in_ref, source, r), high_ref[r], low_ref[r])
        for r in range(4)
    ]
    a, b, c, d = products
    even_sum, even_difference = a + c, a - c
    odd_sum, odd_difference = b + d, sign * turned(b - d)
    quarters = (
        even_sum + odd_sum,
        even_difference + odd_difference,
        even_sum - odd_sum,
        even_difference - odd_difference,
    )
    store_blocks(out_ref, target, quarters)


def spread_left(matrix):
    rest = matrix - matrix.astype(bf16).astype(f32)
    return jnp.concatenate([matrix, rest, matrix], axis=1).astype(bf16)


def three(matrix, right):
    high, low = split(right)
    return mul(spread_left(matrix), jnp.concatenate([high, high, low], axis=0))


def operator_kernel(
    columns_ref, blocks_ref, diag_ref, off_ref, place_ref, owner_ref, pick_ref, out_ref, hold_ref
):
    groups = blocks_ref.shape[0]
    place = place_ref[...]
    owner = owner_ref[...]

    def rows(i):
        return slice(BLOCK * i, BLOCK * i + BLOCK)

    for i in range(4):
        for g in range(groups):
            matrix = blocks_ref[g, i].reshape(2 * BLOCK, BLOCK)
            rest = matrix - matrix.astype(bf16).astype(f32)
            spread = mul(jnp.concatenate([matrix, rest], axis=1).astype(bf16), place)
            hold_ref[g, rows(i), :] = jnp.where(
                owner == columns_ref[g, 2 * i], spread[:BLOCK], 0.0
            ) + jnp.where(owner == columns_ref[g, 2 * i + 1], spread[BLOCK:], 0.0)
    for half, order in ((0, (0, 1, 2, 3)), (1, (3, 2, 1, 0))):
        for step, i in enumerate(order):
            if step:
                last = order[step - 1]
                coupled = min(i, last)
                for g in range(groups):
                    hold_ref[g, rows(i), :] -= three(
                        off_ref[g, half, coupled], hold_ref[g, rows(last), :]
                    )
            for g in range(groups):
                hold_ref[g, rows(i), :] = three(diag_ref[g, half, i], hold_ref[g, rows(i), :])
    pick = pick_ref[...]
    for g in range(groups):
        high, low = split(hold_ref[g])
        ordered = mul(pick, jnp.concatenate([high, low], axis=1))
        out_ref[g] = ordered.astype(bf16)


def apply_kernel(in_ref, operator_ref, out_ref):
    slabs = in_ref.shape[0] // 32
    first = lane_index((LANES, LANES)) < 64
    wide = []
    for r in range(8):
        parts = [in_ref[pl.ds(4 * r + i, slabs, stride=32), :] for i in range(4)]
        high, low = split(jnp.concatenate(swap_groups(parts), axis=0))
        upper = jnp.concatenate([high, low], axis=1)
        lower = jnp.concatenate([high, jnp.zeros_like(low)], axis=1)
        wide.append(jnp.concatenate([upper, lower], axis=0))
    solved = []
    for r in range(8):
        both = mul(operator_ref[2 * r : 2 * r + 2].reshape(2 * LANES, 2 * LANES), wide[r])
        both = both[:, :LANES] + both[:, LANES:]
        solved.append(jnp.where(first, both[:LANES], both[LANES:]))
    for r in range(8):
        parts = swap_groups([solved[r][32 * level : 32 * level + 32] for level in range(4)])
        for i in range(4):
            out_ref[pl.ds(4 * r + i, slabs, stride=32), :] = parts[i]


def call(kernel, shape, *operands, dtype=f32, spaces=None, out=None, scratch=(), flops=0):
    spaces = spaces or [None] * len(operands)
    read = sum(math.prod(o.shape) * o.dtype.itemsize for o in operands)
    operands = [
        operand if space in (None, pltpu.SMEM) else pltpu.with_memory_space_constraint(operand, space)
        for space, operand in zip(spaces, operands)
    ]
    return pl.pallas_call(
        kernel,
        out_shape=jax.ShapeDtypeStruct(shape, dtype),
        in_specs=[pl.BlockSpec(memory_space=space or pltpu.VMEM) for space in spaces],
        out_specs=pl.BlockSpec(memory_space=out or pltpu.VMEM),
        scratch_shapes=scratch,
        cost_estimate=pl.CostEstimate(flops=flops, bytes_accessed=read, transcendentals=0),
        compiler_params=pltpu.CompilerParams(vmem_limit_bytes=VMEM_LIMIT),
    )(*operands)


def exchange(values, axis, order=None):
    members = None if order is None else [order]
    return lax.all_to_all(
        values, axis, split_axis=0, concat_axis=0, axis_index_groups=members, tiled=True
    )


def body(grid_field, operator_blocks, op_columns, diag_inverse, off_blocks):
    depth, lines, length = grid_field.shape
    groups = operator_blocks.shape[1]
    forward_x, backward_x = x_tables()
    forward_y, backward_y = y_tables()
    square = (BLOCK, BLOCK)
    operator = call(
        operator_kernel,
        (groups, LANES, 2 * LANES),
        op_columns.reshape(groups, 8),
        operator_blocks.reshape((groups, 4, 2) + square),
        diag_inverse.reshape((groups, 2, 4) + square),
        off_blocks.reshape((groups, 2, 3) + square),
        *operator_tables(SLABS_THERE, SLABS_BACK),
        dtype=bf16,
        spaces=[pltpu.SMEM] + [None] * 6,
        scratch=[pltpu.VMEM((groups, LANES, LANES), f32)],
        flops=2 * 3 * groups * 22 * BLOCK * BLOCK * LANES,
    )
    x_flops = 2 * 3 * depth * lines * length * HALF
    y_flops = 2 * 3 * 4 * QUARTER * 2 * QUARTER * LANES
    values = call(
        functools.partial(x_forward_kernel, LINES_THERE),
        (16, lines, LANES),
        grid_field,
        *forward_x,
        spaces=[pltpu.HBM] * 3,
        scratch=[
            pltpu.VMEM(grid_field.shape, f32),
            pltpu.VMEM((2, HALF, HALF), bf16),
            pltpu.VMEM((2, HALF, HALF), bf16),
            pltpu.SemaphoreType.DMA((2 + depth,)),
        ],
        flops=x_flops,
    )
    values = exchange(values, "gx", LINES_THERE).reshape(NY, LANES)
    values = call(
        functools.partial(y_kernel, 1.0, LINES_THERE, SLABS_THERE), (NY, LANES), values, *forward_y, flops=y_flops
    )
    values = exchange(values.reshape(32, 32, LANES), "gy", SLABS_THERE).reshape(NY, LANES)
    values = call(
        apply_kernel,
        (NY, LANES),
        values,
        operator,
        flops=2 * 3 * groups * LANES * LANES * LANES,
    )
    values = exchange(values.reshape(32, 32, LANES), "gy", SLABS_BACK).reshape(NY, LANES)
    values = call(
        functools.partial(y_kernel, -1.0, SLABS_BACK, LINES_BACK), (NY, LANES), values, *backward_y, flops=y_flops
    )
    values = exchange(values.reshape(16, lines, LANES), "gx", LINES_BACK)
    return call(
        functools.partial(x_backward_kernel, LINES_BACK),
        (depth, lines, length),
        values,
        *backward_x,
        out=pl.ANY,
        scratch=[pltpu.VMEM((depth, lines, length), f32), pltpu.SemaphoreType.DMA((depth,))],
        flops=x_flops,
    )


def solution(mesh):
    placed = (
        P("gy", "gx", None),
        P("gx", "gy", None, None, None),
        P("gx", "gy", None, None),
        P("gx", "gy", None, None, None),
        P("gx", "gy", None, None, None),
    )
    return jax.shard_map(
        body, mesh=mesh, in_specs=placed, out_specs=P("gy", "gx", None), check_vma=False
    )
```

```python
import functools
import math

import jax
import jax.numpy as jnp
import ml_dtypes
import numpy as np
from jax import lax
from jax.experimental import pallas as pl
from jax.experimental.pallas import tpu as pltpu
from jax.sharding import PartitionSpec as P

NX = 512
NY = 1024
QUARTER = NY // 4
HALF = NX // 2
LANES = 128
SPAN = 16
BLOCK = 32
PART = SPAN // 2
VMEM_LIMIT = 24 * 1024 * 1024

f32 = jnp.float32
bf16 = jnp.bfloat16


def split_table(table):
    high = table.astype(ml_dtypes.bfloat16)
    low = (table - high.astype(np.float64)).astype(ml_dtypes.bfloat16)
    return high, low


def x_tables():
    parity = np.arange(2).reshape(2, 1, 1)
    x = np.arange(HALF).reshape(1, HALF, 1)
    k = 2 * np.arange(HALF // 2).reshape(1, 1, HALF // 2) + parity
    angle = (x * k % NX) * (2.0 * math.pi / NX)
    shape = (2, HALF, HALF // SPAN, PART)
    cosine = np.cos(angle).reshape(shape) / math.sqrt(NX)
    sine = np.sin(angle).reshape(shape) / math.sqrt(NX)
    forward = np.stack([cosine, -sine], axis=3)
    weight = np.where(k == 0, 1.0, 2.0).reshape(2, 1, HALF // SPAN, 1, PART)
    backward = (forward * weight).reshape(2, HALF, HALF).transpose(0, 2, 1)
    return split_table(forward.reshape(2, HALF, HALF)), split_table(backward)


def y_tables():
    residue = np.arange(4).reshape(4, 1, 1)
    row = np.arange(QUARTER).reshape(1, QUARTER, 1)
    j = np.arange(QUARTER).reshape(1, 1, QUARTER)
    angle = (row * (residue + 4 * j) % NY) * (2.0 * math.pi / NY)
    cosine = np.cos(angle) / math.sqrt(NY)
    sine = np.sin(angle) / math.sqrt(NY)
    forward = np.concatenate([cosine, sine], axis=2)
    backward = np.concatenate([cosine, -sine], axis=2)
    return split_table(forward), split_table(backward)


def slab_order(highs, cores, levels):
    return [(8 * high + z) * 2 + core for high in highs for core in cores for z in levels]


def line_order(along_x, along_y):
    return [4 * y + x for x in along_x for y in along_y]


SLABS_THERE = slab_order((1, 0), (1, 0), (7, 6, 5, 4, 3, 2, 1, 0))
SLABS_BACK = slab_order((1, 0), (1, 0), (7, 0, 1, 2, 3, 4, 5, 6))
LINES_THERE = line_order((2, 1, 3, 0), (1, 2, 3, 0))
LINES_BACK = line_order((1, 3, 2, 0), (2, 1, 0, 3))


def operator_tables(there, back):
    def levels(order):
        lane = np.arange(4 * len(order))
        return 4 * np.array(order)[lane % len(order)] + lane // len(order)

    column, line = levels(there), levels(back)
    row = np.arange(BLOCK).reshape(BLOCK, 1)
    place = np.tile(column % BLOCK == row, (2, 1)).astype(ml_dtypes.bfloat16)
    owner = np.broadcast_to(column // BLOCK, (BLOCK, len(column))).astype(np.int32)
    pick = (line.reshape(-1, 1) == np.arange(len(line))).astype(ml_dtypes.bfloat16)
    return place, owner, pick


def split(values):
    high = values.astype(bf16)
    low = (values - high.astype(f32)).astype(bf16)
    return high, low


def mul(left, right):
    return jnp.dot(left, right, preferred_element_type=f32)


def lane_index(shape):
    return lax.broadcasted_iota(jnp.int32, shape, len(shape) - 1)


def swap_groups(parts):
    parts = list(parts)
    lane = lane_index(parts[0].shape)
    distance, reach = len(parts) // 2, LANES // 2
    while distance:
        first = (lane & reach) == 0
        for i in range(len(parts)):
            if not i & distance:
                a, b = parts[i], parts[i + distance]
                parts[i] = jnp.where(first, a, pltpu.roll(b, reach, 1))
                parts[i + distance] = jnp.where(first, pltpu.roll(a, LANES - reach, 1), b)
        distance, reach = distance // 2, reach // 2
    return parts


def turned(values):
    real = (lane_index(values.shape) & PART) == 0
    return jnp.where(real, pltpu.roll(values, LANES - PART, 1), -pltpu.roll(values, PART, 1))


def x_forward_kernel(order, grid_hbm, high_hbm, low_hbm, out_ref, grid_ref, high_ref, low_ref, sems):
    depth, lines, length = grid_ref.shape
    levels = [(grid_hbm.at[z], grid_ref.at[z]) for z in range(depth)]
    half = depth // 2
    pairs = [(high_hbm, high_ref), *levels, (low_hbm, low_ref)]
    copies = [
        pltpu.make_async_copy(source, target, sems.at[i])
        for i, (source, target) in enumerate(pairs)
    ]
    for copy in copies:
        copy.start()
    rows = lines * half
    sums = [[], []]
    for part in range(2):
        for copy in copies[1:][part * half : (part + 1) * half] if part else copies[: 1 + half]:
            copy.wait()
        window = slice(part * half, (part + 1) * half)
        near = grid_ref[window, :, :HALF].reshape(rows, HALF)
        far = grid_ref[window, :, HALF:].reshape(rows, HALF)
        for p, values in enumerate((near + far, near - far)):
            high, low = split(values)
            wide = mul(jnp.concatenate([high, low], axis=0), high_ref[p])
            sums[p].append((high, wide[:rows] + wide[rows:]))
    copies[-1].wait()
    sums = [
        jnp.concatenate([total + mul(high, low_ref[p]) for high, total in sums[p]], axis=0)
        for p in range(2)
    ]
    for a in range(HALF // LANES):
        columns = slice(a * LANES, (a + 1) * LANES)
        parts = [
            sums[p][z * lines : (z + 1) * lines, columns] for z in range(depth) for p in range(2)
        ]
        for b, part in enumerate(swap_groups(parts)):
            out_ref[order.index(8 * a + b)] = part


def x_backward_kernel(order, in_ref, high_ref, low_ref, out_hbm, out_ref, sems):
    depth, lines, length = out_ref.shape
    columns = [
        swap_groups([in_ref[order.index(8 * a + b)] for b in range(8)])
        for a in range(HALF // LANES)
    ]
    step = 2
    copies = []
    for z in range(0, depth, step):
        levels = range(z, z + step)
        results = []
        for p in range(2):
            rows = [
                jnp.concatenate([column[2 * level + p] for column in columns], axis=1)
                for level in levels
            ]
            high, low = split(jnp.concatenate(rows, axis=0))
            wide = mul(jnp.concatenate([high, low], axis=0), high_ref[p])
            count = step * lines
            results.append(wide[:count] + (wide[count:] + mul(high, low_ref[p])))
        near, far = results
        out_ref[z : z + step, :, :HALF] = (near + far).reshape(step, lines, HALF)
        out_ref[z : z + step, :, HALF:] = (near - far).reshape(step, lines, HALF)
        for level in levels:
            copy = pltpu.make_async_copy(out_ref.at[level], out_hbm.at[level], sems.at[level])
            copy.start()
            copies.append(copy)
    for copy in copies:
        copy.wait()


def quarter_product(values, high_table, low_table):
    both = jnp.concatenate([values, turned(values)], axis=0)
    high, low = split(both)
    wide = mul(high_table, jnp.concatenate([high, low], axis=1))
    return wide[:, :LANES] + (wide[:, LANES:] + mul(low_table, high))


def load_blocks(ref, order, r):
    block = ref.shape[0] // len(order)
    parts = [
        ref[pl.ds(block * order.index(i) + r, block // 4, stride=4), :] for i in range(len(order))
    ]
    return jnp.concatenate(parts, axis=0)


def store_blocks(ref, order, quarters):
    block = ref.shape[0] // len(order)
    for place, i in enumerate(order):
        start = block * i % QUARTER
        part = quarters[block * i // QUARTER][start : start + block]
        ref[block * place : block * place + block, :] = part


def y_kernel(sign, source, target, in_ref, high_ref, low_ref, out_ref):
    products = [
        quarter_product(load_blocks(in_ref, source, r), high_ref[r], low_ref[r])
        for r in range(4)
    ]
    a, b, c, d = products
    even_sum, even_difference = a + c, a - c
    odd_sum, odd_difference = b + d, sign * turned(b - d)
    quarters = (
        even_sum + odd_sum,
        even_difference + odd_difference,
        even_sum - odd_sum,
        even_difference - odd_difference,
    )
    store_blocks(out_ref, target, quarters)


def spread_left(matrix):
    rest = matrix - matrix.astype(bf16).astype(f32)
    return jnp.concatenate([matrix, rest, matrix], axis=1).astype(bf16)


def three(matrix, right):
    high, low = split(right)
    return mul(spread_left(matrix), jnp.concatenate([high, high, low], axis=0))


def operator_kernel(
    columns_ref, blocks_ref, diag_ref, off_ref, place_ref, owner_ref, pick_ref, out_ref, hold_ref
):
    groups = blocks_ref.shape[0]
    place = place_ref[...]
    owner = owner_ref[...]

    def rows(i):
        return slice(BLOCK * i, BLOCK * i + BLOCK)

    for i in range(4):
        for g in range(groups):
            matrix = blocks_ref[g, i].reshape(2 * BLOCK, BLOCK)
            rest = matrix - matrix.astype(bf16).astype(f32)
            spread = mul(jnp.concatenate([matrix, rest], axis=1).astype(bf16), place)
            hold_ref[g, rows(i), :] = jnp.where(
                owner == columns_ref[g, 2 * i], spread[:BLOCK], 0.0
            ) + jnp.where(owner == columns_ref[g, 2 * i + 1], spread[BLOCK:], 0.0)
    for half, order in ((0, (0, 1, 2, 3)), (1, (3, 2, 1, 0))):
        for step, i in enumerate(order):
            if step:
                last = order[step - 1]
                coupled = min(i, last)
                for g in range(groups):
                    hold_ref[g, rows(i), :] -= three(
                        off_ref[g, half, coupled], hold_ref[g, rows(last), :]
                    )
            for g in range(groups):
                hold_ref[g, rows(i), :] = three(diag_ref[g, half, i], hold_ref[g, rows(i), :])
    pick = pick_ref[...]
    for g in range(groups):
        high, low = split(hold_ref[g])
        ordered = mul(pick, jnp.concatenate([high, low], axis=1))
        out_ref[g] = ordered.astype(bf16)


def apply_kernel(in_ref, operator_ref, out_ref):
    slabs = in_ref.shape[0] // 32
    first = lane_index((LANES, LANES)) < 64
    wide = []
    for r in range(8):
        parts = [in_ref[pl.ds(4 * r + i, slabs, stride=32), :] for i in range(4)]
        high, low = split(jnp.concatenate(swap_groups(parts), axis=0))
        upper = jnp.concatenate([high, low], axis=1)
        lower = jnp.concatenate([high, jnp.zeros_like(low)], axis=1)
        wide.append(jnp.concatenate([upper, lower], axis=0))
    solved = []
    for r in range(8):
        both = mul(operator_ref[2 * r : 2 * r + 2].reshape(2 * LANES, 2 * LANES), wide[r])
        both = both[:, :LANES] + both[:, LANES:]
        solved.append(jnp.where(first, both[:LANES], both[LANES:]))
    for r in range(8):
        parts = swap_groups([solved[r][32 * level : 32 * level + 32] for level in range(4)])
        for i in range(4):
            out_ref[pl.ds(4 * r + i, slabs, stride=32), :] = parts[i]


def call(kernel, shape, *operands, dtype=f32, spaces=None, out=None, scratch=(), flops=0):
    spaces = spaces or [None] * len(operands)
    read = sum(math.prod(o.shape) * o.dtype.itemsize for o in operands)
    operands = [
        operand if space in (None, pltpu.SMEM) else pltpu.with_memory_space_constraint(operand, space)
        for space, operand in zip(spaces, operands)
    ]
    return pl.pallas_call(
        kernel,
        out_shape=jax.ShapeDtypeStruct(shape, dtype),
        in_specs=[pl.BlockSpec(memory_space=space or pltpu.VMEM) for space in spaces],
        out_specs=pl.BlockSpec(memory_space=out or pltpu.VMEM),
        scratch_shapes=scratch,
        cost_estimate=pl.CostEstimate(flops=flops, bytes_accessed=read, transcendentals=0),
        compiler_params=pltpu.CompilerParams(vmem_limit_bytes=VMEM_LIMIT),
    )(*operands)


def exchange(values, axis, order=None):
    members = None if order is None else [order]
    return lax.all_to_all(
        values, axis, split_axis=0, concat_axis=0, axis_index_groups=members, tiled=True
    )


def body(grid_field, operator_blocks, op_columns, diag_inverse, off_blocks):
    depth, lines, length = grid_field.shape
    groups = operator_blocks.shape[1]
    forward_x, backward_x = x_tables()
    forward_y, backward_y = y_tables()
    square = (BLOCK, BLOCK)
    operator = call(
        operator_kernel,
        (groups, LANES, 2 * LANES),
        op_columns.reshape(groups, 8),
        operator_blocks.reshape((groups, 4, 2) + square),
        diag_inverse.reshape((groups, 2, 4) + square),
        off_blocks.reshape((groups, 2, 3) + square),
        *operator_tables(SLABS_THERE, SLABS_BACK),
        dtype=bf16,
        spaces=[pltpu.SMEM] + [None] * 6,
        scratch=[pltpu.VMEM((groups, LANES, LANES), f32)],
        flops=2 * 3 * groups * 22 * BLOCK * BLOCK * LANES,
    )
    x_flops = 2 * 3 * depth * lines * length * HALF
    y_flops = 2 * 3 * 4 * QUARTER * 2 * QUARTER * LANES
    values = call(
        functools.partial(x_forward_kernel, LINES_THERE),
        (16, lines, LANES),
        grid_field,
        *forward_x,
        spaces=[pltpu.HBM] * 3,
        scratch=[
            pltpu.VMEM(grid_field.shape, f32),
            pltpu.VMEM((2, HALF, HALF), bf16),
            pltpu.VMEM((2, HALF, HALF), bf16),
            pltpu.SemaphoreType.DMA((2 + depth,)),
        ],
        flops=x_flops,
    )
    values = exchange(values, "gx", LINES_THERE).reshape(NY, LANES)
    values = call(
        functools.partial(y_kernel, 1.0, LINES_THERE, SLABS_THERE), (NY, LANES), values, *forward_y, flops=y_flops
    )
    values = exchange(values.reshape(32, 32, LANES), "gy", SLABS_THERE).reshape(NY, LANES)
    values = call(
        apply_kernel,
        (NY, LANES),
        values,
        operator,
        flops=2 * 3 * groups * LANES * LANES * LANES,
    )
    values = exchange(values.reshape(32, 32, LANES), "gy", SLABS_BACK).reshape(NY, LANES)
    values = call(
        functools.partial(y_kernel, -1.0, SLABS_BACK, LINES_BACK), (NY, LANES), values, *backward_y, flops=y_flops
    )
    values = exchange(values.reshape(16, lines, LANES), "gx", LINES_BACK)
    return call(
        functools.partial(x_backward_kernel, LINES_BACK),
        (depth, lines, length),
        values,
        *backward_x,
        out=pl.ANY,
        scratch=[pltpu.VMEM((depth, lines, length), f32), pltpu.SemaphoreType.DMA((depth,))],
        flops=x_flops,
    )


def solution(mesh):
    placed = (
        P("gy", "gx", None),
        P("gx", "gy", None, None, None),
        P("gx", "gy", None, None),
        P("gx", "gy", None, None, None),
        P("gx", "gy", None, None, None),
    )
    return jax.shard_map(
        body, mesh=mesh, in_specs=placed, out_specs=P("gy", "gx", None), check_vma=False
    )
```
